256 devices in a mesh: row: 8 (over y, core), col: 32 (over x, z).
Axes of the slice: x: 4, y: 4, z: 8, core: 2. Of those that a mesh axis runs over, the one named last changes fastest.
Arguments:
- slab: float32 [12288, 20480], P('row', 'col'), may hold values from -6 to 6
- reflectors: bfloat16 [4, 32, 256, 128], P(None, 'col'), may hold values from -0.375 to 0.375
- wy_factors: bfloat16 [4, 32, 128, 128], P(None, 'col'), as said below
- offsets: int32 [4, 32], replicated, may hold values from 0 to 12032, as said below
- band_owner: int32 [4, 32], replicated, may hold values from 0 to 31, each once within a row
Outputs:
- back_vectors: float32 [12288, 20480], P('row', 'col')
The draws below stay inside these ranges and needn't reach their ends.
Inputs may be any that keep to these rules, and one draw needn't show every extreme that they name: In each sweep the offsets rise, each block's 256 rows end before the next block begins, the first block begins at row 0 and the last ends at row 12288; each multiple of 1536 strictly between 0 and 12288 lies strictly inside one block. `band_owner`: each row is a permutation of 0 to 31. `wy_factors`: each factor is upper triangular.
All inputs are finite; a program needn't handle non-finite values.
Results may differ from the reference program's by a relative error of at most 0.0003.
Values may be sent and summed in bfloat16 or wider, within the bound.
A program may use at most 128 MiB of HBM per device.

```python
import jax
import jax.numpy as jnp
from jax import lax

NB = 128
LEN = 256
COLS = 20480
ROWS_DEV = 1536
SWEEPS = 4
BLOCKS = 32
NROWS = 12288
N_ROW = 8


def draw_wy_factors(key, part):
    shape = (SWEEPS, BLOCKS, NB, NB)
    values = jax.random.normal(key, shape, jnp.float32)
    upper = (lax.broadcasted_iota(jnp.int32, shape, 2) <= lax.broadcasted_iota(jnp.int32, shape, 3)).astype(jnp.float32)
    return (values * upper * (1.0 / math_sqrt(NB))).astype(jnp.bfloat16)


def math_sqrt(value):
    return float(value) ** 0.5


def draw_offsets(key, part):
    key = jax.random.fold_in(key, 7)
    group = BLOCKS // N_ROW
    below = jax.random.randint(jax.random.fold_in(key, 1), (SWEEPS, N_ROW - 1), 1, LEN).astype(jnp.int32)
    bounds = jnp.arange(1, N_ROW, dtype=jnp.int32)[None, :] * ROWS_DEV
    starts = jnp.concatenate([jnp.zeros((SWEEPS, 1), jnp.int32), bounds - below], axis=1)
    ends = jnp.concatenate([starts[:, 1:], jnp.full((SWEEPS, 1), NROWS, jnp.int32)], axis=1)
    room = ends - starts - group * LEN
    inner = jax.random.randint(jax.random.fold_in(key, 2), (SWEEPS, N_ROW, group - 1), 0, room[:, :, None] + 1).astype(jnp.int32)
    inner = jnp.sort(inner, axis=2)
    shifts = jnp.concatenate([jnp.zeros((SWEEPS, N_ROW, 1), jnp.int32), inner], axis=2)
    shifts = shifts.at[:, N_ROW - 1, group - 1].set(room[:, N_ROW - 1])
    within = jnp.arange(group, dtype=jnp.int32)[None, None, :] * LEN
    placed = starts[:, :, None] + within + shifts
    return placed.reshape(SWEEPS, BLOCKS).astype(jnp.int32)


def level_of(own_key, extent, cuts, low, high):
    factor_of = 1.0
    for axis_at, blocks in cuts:
        steps = jax.random.uniform(jax.random.fold_in(jax.random.fold_in(own_key, 6), axis_at), (blocks,), jnp.float32, low / len(cuts), high / len(cuts))
        factor_of = factor_of * jnp.repeat(jnp.exp(steps), extent[axis_at] // blocks).reshape((-1,) + (1,) * (len(extent) - 1 - axis_at))
    return factor_of


def bell_draw(rng, shape, spread, reach, shards=(), kind=jnp.bfloat16):
    result = jax.random.normal(rng, shape, jnp.float32) * spread
    if len(shards) > 0:
        result = level_of(rng, shape, shards, -0.22, 0.18) * result
    return jnp.clip(result, min=-reach, max=reach).astype(kind)


def setup_inputs(seed: int = 0) -> dict:
    keys = jax.random.split(jax.random.key(seed), 6)
    return {
        "slab": bell_draw(keys[0], (NROWS, COLS), 1.0, 6.0, ((0, 8), (1, 32)), jnp.float32),
        "reflectors": bell_draw(keys[1], (SWEEPS, BLOCKS, LEN, NB), LEN ** -0.5, 0.375, ((1, 32),)),
        "wy_factors": draw_wy_factors(jax.random.fold_in(keys[5], 71), 0),
        "offsets": draw_offsets(jax.random.fold_in(keys[5], 71), 0),
        "band_owner": jax.vmap(lambda own: jax.random.permutation(own, BLOCKS))(jax.random.split(keys[4], SWEEPS)).reshape((SWEEPS, BLOCKS)).astype(jnp.int32),
    }


def reference(slab, reflectors, wy_factors, offsets, band_owner):
    state = slab
    for sweep_index in range(SWEEPS):
        def apply_block(block_index, current):
            holder = band_owner[sweep_index, block_index]
            begin = offsets[sweep_index, block_index]
            vblock = lax.dynamic_index_in_dim(reflectors[sweep_index], holder, 0, keepdims=False).astype(jnp.float32)
            factor = lax.dynamic_index_in_dim(wy_factors[sweep_index], holder, 0, keepdims=False).astype(jnp.float32)
            block_rows = lax.dynamic_slice_in_dim(current, begin, LEN, 0)
            inner = jnp.dot(vblock.T, block_rows, precision=lax.Precision.HIGHEST, preferred_element_type=jnp.float32)
            scaled = jnp.dot(factor, inner, precision=lax.Precision.HIGHEST, preferred_element_type=jnp.float32)
            updated = block_rows - jnp.dot(vblock, scaled, precision=lax.Precision.HIGHEST, preferred_element_type=jnp.float32)
            return lax.dynamic_update_slice_in_dim(current, updated, begin, 0)

        state = lax.fori_loop(0, BLOCKS, apply_block, state)
    return state
```

```python
import functools

import jax
import jax.numpy as jnp
from jax import lax
from jax.experimental import pallas as pl
from jax.experimental.pallas import tpu as pltpu
from jax.sharding import PartitionSpec as P

SWEEPS = 4
LEN = 256
NB = 128
SLOTS = 7
TILES = 6
ZX = 4
BLK = LEN + NB
MESH = pl.DeviceIdType.MESH
F32 = jnp.float32
BF16 = jnp.bfloat16


def split(value):
    high = value.astype(BF16)
    low = (value - high.astype(F32)).astype(BF16)
    return high, low


def dot(left, right):
    return jnp.dot(left, right, preferred_element_type=F32)


def kernel(nx, nz, nrow, tab, slab, refl, fact, out, x, own, pieces, blocks, vt, wbuf, wrec,
           load_sem, store_sem, a2a_sem, zx_send, zx_recv, xs_send, xs_recv, xz_send, xz_recv, zs_send, zs_recv,
           w_send, w_recv):
    ncol = nx * nz
    me = lax.axis_index("col")
    row = lax.axis_index("row")
    mx, mz = me // nz, me % nz
    piece = BLK // nz
    cols = x.shape[1]
    loads = pltpu.make_async_copy(slab, x, load_sem)
    loads.start()

    right_row, left_row = (row + 1) % nrow, (row + nrow - 1) % nrow
    barrier = pltpu.get_barrier_semaphore()

    def greet(k, carry):
        pl.semaphore_signal(barrier, inc=1, device_id={"col": (me + k) % ncol}, device_id_type=MESH)
        return carry

    lax.fori_loop(1, ncol, greet, 0)
    pl.semaphore_signal(barrier, inc=1, device_id={"row": right_row}, device_id_type=MESH)
    pl.semaphore_signal(barrier, inc=1, device_id={"row": left_row}, device_id_type=MESH)

    ri = lax.broadcasted_iota(jnp.int32, (LEN, LEN), 0)
    ci = lax.broadcasted_iota(jnp.int32, (LEN, LEN), 1)
    for s in range(SWEEPS):
        place = (((ri - tab[s, 24]) & (LEN - 1)) == ci).astype(BF16)
        own[s, pl.ds(0, LEN), :] = dot(place, refl[s, 0]).astype(BF16)
        own[s, pl.ds(LEN, NB), :] = fact[s, 0]

    pl.semaphore_wait(barrier, ncol + 1)

    def send_piece(k, carry):
        to = (me + k) % ncol
        pltpu.make_async_remote_copy(
            src_ref=own.at[to // nz, pl.ds(pl.multiple_of((to % nz) * piece, 16), piece), :],
            dst_ref=pieces.at[me],
            send_sem=a2a_sem.at[0],
            recv_sem=a2a_sem.at[1],
            device_id={"col": to},
            device_id_type=MESH,
        ).start()
        return carry

    lax.fori_loop(1, ncol, send_piece, 0)
    my_rows = pl.ds(pl.multiple_of(mz * piece, 16), piece)
    pieces[me] = own[mx, my_rows, :]
    everything = pieces.at[pl.ds(0, ncol - 1)]
    pltpu.make_async_copy(everything, everything, a2a_sem.at[1]).wait()
    for t in range(SLOTS):
        found = pieces[tab[mx, 8 + t]].astype(F32) * tab[mx, 16 + t].astype(F32)
        blocks[mx, t, my_rows, :] = found.astype(BF16)
    pltpu.make_async_copy(everything, everything, a2a_sem.at[0]).wait()

    def col_of(cx, cz):
        return ((cx + nx) % nx) * nz + (cz + nz) % nz

    def rows_of(cz):
        return pl.ds(pl.multiple_of(((cz + nz) % nz) * piece, 16), piece)

    def move(part, to, send, recv):
        copy = pltpu.make_async_remote_copy(
            src_ref=part, dst_ref=part, send_sem=send, recv_sem=recv, device_id={"col": to}, device_id_type=MESH)
        copy.start()
        return copy

    first = pl.ds(0, ZX)
    second = pl.ds(ZX, SLOTS - ZX)
    n_cw, n_ccw = nz // 2, (nz - 1) // 2
    sent = []

    def zx_step(k, way):
        part = blocks.at[mx, first, rows_of(mz - way * k), :]
        i = k if way > 0 else n_cw + k
        copy = move(part, col_of(mx, mz + way), zx_send.at[i], zx_recv.at[i])
        sent.append(copy)
        return copy

    def zs_step(k, way):
        part = blocks.at[:, second, rows_of(mz - way * k), :]
        i = k if way > 0 else n_cw + k
        copy = move(part, col_of(mx, mz + way), zs_send.at[i], zs_recv.at[i])
        sent.append(copy)
        return copy

    mine = blocks.at[mx, second, my_rows, :]
    xz = [move(mine, col_of(mx + k, mz), xz_send.at[k - 1], xz_recv.at[k - 1]) for k in range(1, nx)]
    sent.extend(xz)
    cw = zx_step(0, 1)
    ccw = zx_step(0, -1) if n_ccw else None
    for copy in xz:
        copy.wait_recv()
    zcw = zs_step(0, 1)
    zccw = zs_step(0, -1) if n_ccw else None
    for k in range(n_cw):
        cw.wait_recv()
        if k + 1 < n_cw:
            cw = zx_step(k + 1, 1)
        if k < n_ccw:
            ccw.wait_recv()
            if k + 1 < n_ccw:
                ccw = zx_step(k + 1, -1)
    xs = [
        move(blocks.at[mx, first], col_of(mx + way, mz), xs_send.at[i], xs_recv.at[i])
        for i, way in enumerate((1, -1))
    ]
    sent.extend(xs)
    half = ZX // 2
    far = []
    for k in range(n_cw):
        zcw.wait_recv()
        if k + 1 < n_cw:
            zcw = zs_step(k + 1, 1)
        if k < n_ccw:
            zccw.wait_recv()
            if k + 1 < n_ccw:
                zccw = zs_step(k + 1, -1)
        if k == n_cw // 2:
            for i, way in enumerate((1, -1)):
                xs[i].wait_recv()
                part = blocks.at[(mx - way + nx) % nx, pl.ds(i * half, half)]
                far.append(move(part, col_of(mx + way, mz), xs_send.at[2 + i], xs_recv.at[2 + i]))
    sent.extend(far)
    for copy in far:
        copy.wait_recv()
    for copy in sent:
        copy.wait_send()
    loads.wait()

    at = lax.broadcasted_iota(jnp.int32, (LEN, 1), 0)

    def inner(v_t, z):
        high, low = split(z)
        return dot(v_t, high) + dot(v_t, low)

    def change(s, t, w):
        f = blocks[s, t, pl.ds(LEN, NB), :]
        v = blocks[s, t, pl.ds(0, LEN), :]
        y = dot(jnp.concatenate([f, f], axis=1), jnp.concatenate(split(w), axis=0))
        return dot(jnp.concatenate([v, v], axis=1), jnp.concatenate(split(y), axis=0))

    def tile(t):
        return pl.ds(pl.multiple_of(t * LEN, LEN), LEN)

    last = pl.ds((TILES - 1) * LEN, LEN)

    def sweep(s, carry):
        for t in range(SLOTS):
            vt[t] = blocks[s, t, pl.ds(0, LEN), :].T
        d_first, d_last = tab[s, 0], tab[s, SLOTS - 1]
        wbuf[0] = inner(vt[0], jnp.where(at < d_first, x[pl.ds(0, LEN), :], 0.0))
        wbuf[1] = inner(vt[SLOTS - 1], jnp.where(at >= d_last, x[last, :], 0.0))
        par = s % 2
        copies = [
            pltpu.make_async_remote_copy(
                src_ref=wbuf.at[side], dst_ref=wrec.at[par, 1 - side], send_sem=w_send.at[side],
                recv_sem=w_recv.at[par, 1 - side], device_id={"row": to}, device_id_type=MESH)
            for side, to in ((0, left_row), (1, right_row))
        ]
        for copy in copies:
            copy.start()

        def body(t, carry):
            d = tab[s, t + 1]
            z = jnp.where(at >= d, x[tile(t), :], x[tile(t + 1), :])
            delta = change(s, t + 1, inner(vt[t + 1], z))
            x[tile(t), :] = x[tile(t), :] - jnp.where(at >= d, delta, 0.0)
            x[tile(t + 1), :] = x[tile(t + 1), :] - jnp.where(at < d, delta, 0.0)
            return carry

        lax.fori_loop(0, TILES - 1, body, 0)
        for copy in copies:
            copy.wait()
        delta = change(s, 0, wbuf[0] + wrec[par, 0])
        x[pl.ds(0, LEN), :] = x[pl.ds(0, LEN), :] - jnp.where(at < d_first, delta, 0.0)
        delta = change(s, SLOTS - 1, wbuf[1] + wrec[par, 1])
        x[last, :] = x[last, :] - jnp.where(at >= d_last, delta, 0.0)
        return carry

    lax.fori_loop(0, SWEEPS, sweep, 0)
    stores = pltpu.make_async_copy(x, out, store_sem)
    stores.start()
    stores.wait()


def tables(offsets, owners):
    row, col = lax.axis_index("row"), lax.axis_index("col")
    begin_tile = offsets // LEN
    within = offsets % LEN
    slot = jnp.arange(8, dtype=jnp.int32) + (row * TILES - 1)
    slot = jnp.where(jnp.arange(8) < SLOTS, slot, -2)
    match = (begin_tile[:, None, :] == slot[None, :, None]).astype(jnp.int32)
    own = jnp.sum((owners == col) * within, axis=1, keepdims=True)
    return jnp.concatenate(
        [
            jnp.sum(match * within[:, None, :], axis=2),
            jnp.sum(match * owners[:, None, :], axis=2),
            jnp.sum(match, axis=2),
            jnp.broadcast_to(own, (SWEEPS, 8)),
        ],
        axis=1,
    ).astype(jnp.int32)


def on_device(nx, nz, nrow, slab, reflectors, factors, offsets, owners):
    cols = slab.shape[1]
    ncol = nx * nz
    dma = pltpu.SemaphoreType.DMA
    n_ring = nz - 1
    return pl.pallas_call(
        functools.partial(kernel, nx, nz, nrow),
        out_shape=jax.ShapeDtypeStruct(slab.shape, F32),
        in_specs=[
            pl.BlockSpec(memory_space=pltpu.SMEM),
            pl.BlockSpec(memory_space=pl.ANY),
            pl.BlockSpec(memory_space=pltpu.VMEM),
            pl.BlockSpec(memory_space=pltpu.VMEM),
        ],
        out_specs=pl.BlockSpec(memory_space=pl.ANY),
        scratch_shapes=[
            pltpu.VMEM(slab.shape, F32),
            pltpu.VMEM((SWEEPS, BLK, NB), BF16),
            pltpu.VMEM((ncol, BLK // nz, NB), BF16),
            pltpu.VMEM((nx, SLOTS, BLK, NB), BF16),
            pltpu.VMEM((SLOTS, NB, LEN), BF16),
            pltpu.VMEM((2, NB, cols), F32),
            pltpu.VMEM((2, 2, NB, cols), F32),
            dma, dma, dma((2,)),
            dma((n_ring,)), dma((n_ring,)),
            dma((4,)), dma((4,)),
            dma((nx - 1,)), dma((nx - 1,)),
            dma((n_ring,)), dma((n_ring,)),
            dma((2,)), dma((2, 2)),
        ],
        compiler_params=pltpu.CompilerParams(
            collective_id=0, has_side_effects=True, vmem_limit_bytes=56 * 2**20
        ),
        cost_estimate=pl.CostEstimate(flops=6_000_000_000, bytes_accessed=9_000_000, transcendentals=0),
    )(tables(offsets, owners), slab, reflectors, factors)


def solution(mesh):
    nx = SWEEPS
    nz = mesh.shape["col"] // nx
    placed = (P("row", "col"), P(None, "col", None, None), P(None, "col", None, None), P(), P())
    return jax.shard_map(
        functools.partial(on_device, nx, nz, mesh.shape["row"]),
        mesh=mesh, in_specs=placed, out_specs=P("row", "col"), check_vma=False,
    )
```

```python
import functools

import jax
import jax.numpy as jnp
from jax import lax
from jax.experimental import pallas as pl
from jax.experimental.pallas import tpu as pltpu
from jax.sharding import PartitionSpec as P

SWEEPS = 4
LEN = 256
NB = 128
SLOTS = 7
TILES = 6
ZX = 4
BLK = LEN + NB
MESH = pl.DeviceIdType.MESH
F32 = jnp.float32
BF16 = jnp.bfloat16


def split(value):
    high = value.astype(BF16)
    low = (value - high.astype(F32)).astype(BF16)
    return high, low


def dot(left, right):
    return jnp.dot(left, right, preferred_element_type=F32)


def kernel(nx, nz, nrow, cut, tab, slab, refl, fact, x, own, pieces, blocks, vt, vpair, ys, wbuf, wrec,
           load_sem, a2a_sem, zx_send, zx_recv, xs_send, xs_recv, xz_send, xz_recv, zs_send, zs_recv,
           w_send, w_recv):
    ncol = nx * nz
    me = lax.axis_index("col")
    row = lax.axis_index("row")
    mx, mz = me // nz, me % nz
    piece = BLK // nz
    cols = x.shape[1]
    loads = pltpu.make_async_copy(slab, x, load_sem)
    loads.start()

    right_row, left_row = (row + 1) % nrow, (row + nrow - 1) % nrow
    barrier = pltpu.get_barrier_semaphore()

    def greet(k, carry):
        pl.semaphore_signal(barrier, inc=1, device_id={"col": (me + k) % ncol}, device_id_type=MESH)
        return carry

    lax.fori_loop(1, ncol, greet, 0)
    pl.semaphore_signal(barrier, inc=1, device_id={"row": right_row}, device_id_type=MESH)
    pl.semaphore_signal(barrier, inc=1, device_id={"row": left_row}, device_id_type=MESH)

    ri = lax.broadcasted_iota(jnp.int32, (LEN, LEN), 0)
    ci = lax.broadcasted_iota(jnp.int32, (LEN, LEN), 1)
    for s in range(SWEEPS):
        place = (((ri - tab[s, 24]) & (LEN - 1)) == ci).astype(BF16)
        own[s, pl.ds(0, LEN), :] = dot(place, refl[s, 0]).astype(BF16)
        own[s, pl.ds(LEN, NB), :] = fact[s, 0]

    pl.semaphore_wait(barrier, ncol + 1)

    def send_piece(k, carry):
        to = (me + k) % ncol
        pltpu.make_async_remote_copy(
            src_ref=own.at[to // nz, pl.ds(pl.multiple_of((to % nz) * piece, 16), piece), :],
            dst_ref=pieces.at[me],
            send_sem=a2a_sem.at[0],
            recv_sem=a2a_sem.at[1],
            device_id={"col": to},
            device_id_type=MESH,
        ).start()
        return carry

    lax.fori_loop(1, ncol, send_piece, 0)
    my_rows = pl.ds(pl.multiple_of(mz * piece, 16), piece)
    pieces[me] = own[mx, my_rows, :]
    everything = pieces.at[pl.ds(0, ncol - 1)]
    pltpu.make_async_copy(everything, everything, a2a_sem.at[1]).wait()
    for t in range(SLOTS):
        found = pieces[tab[mx, 8 + t]].astype(F32) * tab[mx, 16 + t].astype(F32)
        blocks[mx, t, my_rows, :] = found.astype(BF16)
    pltpu.make_async_copy(everything, everything, a2a_sem.at[0]).wait()

    def col_of(cx, cz):
        return ((cx + nx) % nx) * nz + (cz + nz) % nz

    def rows_of(cz):
        return pl.ds(pl.multiple_of(((cz + nz) % nz) * piece, 16), piece)

    def move(part, to, send, recv):
        copy = pltpu.make_async_remote_copy(
            src_ref=part, dst_ref=part, send_sem=send, recv_sem=recv, device_id={"col": to}, device_id_type=MESH)
        copy.start()
        return copy

    first = pl.ds(0, ZX)
    second = pl.ds(ZX, SLOTS - ZX)
    n_cw, n_ccw = nz // 2, (nz - 1) // 2
    sent = []

    def zx_step(k, way):
        part = blocks.at[mx, first, rows_of(mz - way * k), :]
        i = k if way > 0 else n_cw + k
        copy = move(part, col_of(mx, mz + way), zx_send.at[i], zx_recv.at[i])
        sent.append(copy)
        return copy

    def zs_step(k, way):
        part = blocks.at[:, second, rows_of(mz - way * k), :]
        i = k if way > 0 else n_cw + k
        copy = move(part, col_of(mx, mz + way), zs_send.at[i], zs_recv.at[i])
        sent.append(copy)
        return copy

    mine = blocks.at[mx, second, my_rows, :]
    xz = [move(mine, col_of(mx + k, mz), xz_send.at[k - 1], xz_recv.at[k - 1]) for k in range(1, nx)]
    sent.extend(xz)
    cw = zx_step(0, 1)
    ccw = zx_step(0, -1) if n_ccw else None
    for copy in xz:
        copy.wait_recv()
    zcw = zs_step(0, 1)
    zccw = zs_step(0, -1) if n_ccw else None
    for k in range(n_cw):
        cw.wait_recv()
        if k + 1 < n_cw:
            cw = zx_step(k + 1, 1)
        if k < n_ccw:
            ccw.wait_recv()
            if k + 1 < n_ccw:
                ccw = zx_step(k + 1, -1)
    xs = [
        move(blocks.at[mx, first], col_of(mx + way, mz), xs_send.at[i], xs_recv.at[i])
        for i, way in enumerate((1, -1))
    ]
    sent.extend(xs)
    half = ZX // 2
    far = []
    for k in range(n_cw):
        zcw.wait_recv()
        if k + 1 < n_cw:
            zcw = zs_step(k + 1, 1)
        if k < n_ccw:
            zccw.wait_recv()
            if k + 1 < n_ccw:
                zccw = zs_step(k + 1, -1)
        if k == n_cw // 2:
            for i, way in enumerate((1, -1)):
                xs[i].wait_recv()
                part = blocks.at[(mx - way + nx) % nx, pl.ds(i * half, half)]
                far.append(move(part, col_of(mx + way, mz), xs_send.at[2 + i], xs_recv.at[2 + i]))
    sent.extend(far)
    for copy in far:
        copy.wait_recv()
    for copy in sent:
        copy.wait_send()
    loads.wait()

    at = lax.broadcasted_iota(jnp.int32, (LEN, 1), 0)
    halves = [(0, cut), (cut, cols - cut)] if cut < cols else [(0, cols)]

    def keep(value, mask):
        return jnp.where(mask, value.astype(F32), 0.0).astype(BF16)

    def tile(t, h):
        return x[pl.ds(t * LEN, LEN), pl.ds(*halves[h])]

    def inner(s, t, h):
        d = tab[s, t]
        if t == 0:
            z = jnp.where(at < d, tile(0, h), 0.0)
        elif t == SLOTS - 1:
            z = jnp.where(at >= d, tile(TILES - 1, h), 0.0)
        else:
            z = jnp.where(at >= d, tile(t - 1, h), tile(t, h))
        high, low = split(z)
        return dot(vt[t], high) + dot(vt[t], low)

    def scale(s, t, h, w):
        f = blocks[s, t, pl.ds(LEN, NB), :]
        y = dot(jnp.concatenate([f, f], axis=1), jnp.concatenate(split(w), axis=0))
        ys[t, :, pl.ds(*halves[h])] = jnp.concatenate(split(y), axis=0)

    def apply(s, t, h):
        here = pl.ds(t * LEN, LEN), pl.ds(*halves[h])
        delta = dot(vpair[t], ys[pl.ds(t, 2), :, pl.ds(*halves[h])].reshape(4 * NB, halves[h][1]))
        x[here] = x[here] - delta

    def exchange(s, h):
        par = s % 2
        part = pl.ds(*halves[h])
        return [
            pltpu.make_async_remote_copy(
                src_ref=wbuf.at[par, side, :, part], dst_ref=wrec.at[par, 1 - side, :, part],
                send_sem=w_send.at[par, side, h], recv_sem=w_recv.at[par, 1 - side, h],
                device_id={"row": to}, device_id_type=MESH)
            for side, to in ((0, left_row), (1, right_row))
        ]

    def edges(s, h):
        wbuf[s % 2, 0, :, pl.ds(*halves[h])] = inner(s, 0, h)
        wbuf[s % 2, 1, :, pl.ds(*halves[h])] = inner(s, SLOTS - 1, h)
        for copy in exchange(s, h):
            copy.start()

    def finish(s, h):
        for copy in exchange(s, h):
            copy.wait()
        part = pl.ds(*halves[h])
        for side, t in ((0, 0), (1, SLOTS - 1)):
            scale(s, t, h, wbuf[s % 2, side, :, part] + wrec[s % 2, side, :, part])
        apply(s, 0, h)
        apply(s, TILES - 1, h)

    def sweep(s, carry):
        for t in range(SLOTS):
            vt[t] = blocks[s, t, pl.ds(0, LEN), :].T
        for h in range(len(halves)):
            edges(s, h)
            for t in range(1, SLOTS - 1):
                scale(s, t, h, inner(s, t, h))
            if h == 0:
                for t in range(TILES):
                    before = keep(blocks[s, t, pl.ds(0, LEN), :], at < tab[s, t])
                    after = keep(blocks[s, t + 1, pl.ds(0, LEN), :], at >= tab[s, t + 1])
                    vpair[t] = jnp.concatenate([before, before, after, after], axis=1)
            for t in range(1, TILES - 1):
                apply(s, t, h)
        for h in range(len(halves)):
            finish(s, h)
        return carry

    lax.fori_loop(0, SWEEPS, sweep, 0)


def tables(offsets, owners):
    row, col = lax.axis_index("row"), lax.axis_index("col")
    begin_tile = offsets // LEN
    within = offsets % LEN
    slot = jnp.arange(8, dtype=jnp.int32) + (row * TILES - 1)
    slot = jnp.where(jnp.arange(8) < SLOTS, slot, -2)
    match = (begin_tile[:, None, :] == slot[None, :, None]).astype(jnp.int32)
    own = jnp.sum((owners == col) * within, axis=1, keepdims=True)
    return jnp.concatenate(
        [
            jnp.sum(match * within[:, None, :], axis=2),
            jnp.sum(match * owners[:, None, :], axis=2),
            jnp.sum(match, axis=2),
            jnp.broadcast_to(own, (SWEEPS, 8)),
        ],
        axis=1,
    ).astype(jnp.int32)


def on_device(nx, nz, nrow, slab, reflectors, factors, offsets, owners):
    cols = slab.shape[1]
    ncol = nx * nz
    dma = pltpu.SemaphoreType.DMA
    n_ring = nz - 1
    return pl.pallas_call(
        functools.partial(kernel, nx, nz, nrow, 384),
        out_shape=pltpu.VMEM(slab.shape, F32),
        in_specs=[
            pl.BlockSpec(memory_space=pltpu.SMEM),
            pl.BlockSpec(memory_space=pl.ANY),
            pl.BlockSpec(memory_space=pltpu.VMEM),
            pl.BlockSpec(memory_space=pltpu.VMEM),
        ],
        out_specs=pl.BlockSpec(memory_space=pltpu.VMEM),
        scratch_shapes=[
            pltpu.VMEM((SWEEPS, BLK, NB), BF16),
            pltpu.VMEM((ncol, BLK // nz, NB), BF16),
            pltpu.VMEM((nx, SLOTS, BLK, NB), BF16),
            pltpu.VMEM((SLOTS, NB, LEN), BF16),
            pltpu.VMEM((TILES, LEN, 4 * NB), BF16),
            pltpu.VMEM((SLOTS, 2 * NB, cols), BF16),
            pltpu.VMEM((2, 2, NB, cols), F32),
            pltpu.VMEM((2, 2, NB, cols), F32),
            dma, dma((2,)),
            dma((n_ring,)), dma((n_ring,)),
            dma((4,)), dma((4,)),
            dma((nx - 1,)), dma((nx - 1,)),
            dma((n_ring,)), dma((n_ring,)),
            dma((2, 2, 2)), dma((2, 2, 2)),
        ],
        compiler_params=pltpu.CompilerParams(
            collective_id=0, has_side_effects=True, vmem_limit_bytes=56 * 2**20
        ),
        cost_estimate=pl.CostEstimate(flops=6_000_000_000, bytes_accessed=9_000_000, transcendentals=0),
    )(tables(offsets, owners), slab, reflectors, factors)


def solution(mesh):
    nx = SWEEPS
    nz = mesh.shape["col"] // nx
    placed = (P("row", "col"), P(None, "col", None, None), P(None, "col", None, None), P(), P())
    return jax.shard_map(
        functools.partial(on_device, nx, nz, mesh.shape["row"]),
        mesh=mesh, in_specs=placed, out_specs=P("row", "col"), check_vma=False,
    )
```

```python
import functools

import jax
import jax.numpy as jnp
from jax import lax
from jax.experimental import pallas as pl
from jax.experimental.pallas import tpu as pltpu
from jax.sharding import PartitionSpec as P

SWEEPS = 4
LEN = 256
NB = 128
SLOTS = 7
TILES = 6
ZX = 4
BLK = LEN + NB
CUT = 384
MESH = pl.DeviceIdType.MESH
F32 = jnp.float32
BF16 = jnp.bfloat16


def split(value):
    high = value.astype(BF16)
    low = (value - high.astype(F32)).astype(BF16)
    return high, low


def dot(left, right):
    return jnp.dot(left, right, preferred_element_type=F32)


def kernel(nx, nz, nrow, cut, tab, slab, refl, fact, x, own, pieces, blocks, vt, vpair, ys, wbuf, wrec,
           load_sem, a2a_sem, zx_send, zx_recv, xs_send, xs_recv, far_send, far_recv, xz_send, xz_recv, zs_send, zs_recv,
           w_send, w_recv):
    ncol = nx * nz
    me = lax.axis_index("col")
    row = lax.axis_index("row")
    mx, mz = me // nz, me % nz
    piece = BLK // nz
    cols = x.shape[1]
    loads = pltpu.make_async_copy(slab, x, load_sem)
    loads.start()

    right_row, left_row = (row + 1) % nrow, (row + nrow - 1) % nrow
    barrier = pltpu.get_barrier_semaphore()

    def greet(k, carry):
        pl.semaphore_signal(barrier, inc=1, device_id={"col": (me + k) % ncol}, device_id_type=MESH)
        return carry

    lax.fori_loop(1, ncol, greet, 0)
    pl.semaphore_signal(barrier, inc=1, device_id={"row": right_row}, device_id_type=MESH)
    pl.semaphore_signal(barrier, inc=1, device_id={"row": left_row}, device_id_type=MESH)

    ri = lax.broadcasted_iota(jnp.int32, (LEN, LEN), 0)
    ci = lax.broadcasted_iota(jnp.int32, (LEN, LEN), 1)
    for s in range(SWEEPS):
        place = (((ri - tab[s, 24]) & (LEN - 1)) == ci).astype(BF16)
        own[s, pl.ds(0, LEN), :] = dot(place, refl[s, 0]).astype(BF16)
        own[s, pl.ds(LEN, NB), :] = fact[s, 0]

    pl.semaphore_wait(barrier, ncol + 1)

    def send_piece(k, carry):
        to = (me + k) % ncol
        pltpu.make_async_remote_copy(
            src_ref=own.at[to // nz, pl.ds(pl.multiple_of((to % nz) * piece, 16), piece), :],
            dst_ref=pieces.at[me],
            send_sem=a2a_sem.at[0],
            recv_sem=a2a_sem.at[1],
            device_id={"col": to},
            device_id_type=MESH,
        ).start()
        return carry

    lax.fori_loop(1, ncol, send_piece, 0)
    my_rows = pl.ds(pl.multiple_of(mz * piece, 16), piece)
    pieces[me] = own[mx, my_rows, :]
    everything = pieces.at[pl.ds(0, ncol - 1)]
    pltpu.make_async_copy(everything, everything, a2a_sem.at[1]).wait()
    for t in range(SLOTS):
        found = pieces[tab[mx, 8 + t]].astype(F32) * tab[mx, 16 + t].astype(F32)
        blocks[mx, t, my_rows, :] = found.astype(BF16)
    pltpu.make_async_copy(everything, everything, a2a_sem.at[0]).wait()

    def col_of(cx, cz):
        return ((cx + nx) % nx) * nz + (cz + nz) % nz

    def rows_of(cz):
        return pl.ds(pl.multiple_of(((cz + nz) % nz) * piece, 16), piece)

    def move(part, to, send, recv):
        copy = pltpu.make_async_remote_copy(
            src_ref=part, dst_ref=part, send_sem=send, recv_sem=recv, device_id={"col": to}, device_id_type=MESH)
        copy.start()
        return copy

    first = pl.ds(0, ZX)
    second = pl.ds(ZX, SLOTS - ZX)
    n_cw, n_ccw = nz // 2, (nz - 1) // 2
    reach = [0] + [-1 - k for k in range(n_cw)] + [1 + k for k in range(n_ccw)]
    sent = []

    def start(part, to, send, recv):
        copy = move(part, to, send, recv)
        sent.append(copy)
        return copy

    def zx_step(k, way):
        i = k if way > 0 else n_cw + k
        return start(blocks.at[mx, first, rows_of(mz - way * k), :], col_of(mx, mz + way), zx_send.at[i], zx_recv.at[i])

    def zs_step(k, way, c):
        i = k if way > 0 else n_cw + k
        part = blocks.at[c, second, rows_of(mz - way * k), :]
        return start(part, col_of(mx, mz + way), zs_send.at[i, c], zs_recv.at[i, c])

    near = [[None] * nz, [None] * nz]

    def near_step(i):
        part = blocks.at[mx, first, rows_of(mz + reach[i]), :]
        for side, way in ((0, 1), (1, -1)):
            near[side][i] = start(part, col_of(mx + way, mz), xs_send.at[side, i], xs_recv.at[side, i])

    order = [0] + [i for k in range(n_cw) for i in ((1 + k, 1 + n_cw + k) if k < n_ccw else (1 + k,))]
    far = []

    def far_step(j):
        for side, way in ((0, 1), (1, -1)):
            i = order[2 * j + side]
            near[side][i].wait_recv()
            near[side][i] = None
            part = blocks.at[(mx - way + nx) % nx, first, rows_of(mz + reach[i]), :]
            far.append(start(part, col_of(mx + way, mz), far_send.at[2 * j + side], far_recv.at[2 * j + side]))

    mine = blocks.at[mx, second, my_rows, :]
    xz = [start(mine, col_of(mx + k, mz), xz_send.at[k - 1], xz_recv.at[k - 1]) for k in range(1, nx)]
    cw = zx_step(0, 1)
    ccw = zx_step(0, -1) if n_ccw else None
    near_step(0)
    for copy in xz:
        copy.wait_recv()
    zcw, zccw = [None] * nx, [None] * nx
    for c in range(nx):
        zcw[c] = zs_step(0, 1, c)
        if n_ccw:
            zccw[c] = zs_step(0, -1, c)
    for k in range(n_cw):
        cw.wait_recv()
        if k + 1 < n_cw:
            cw = zx_step(k + 1, 1)
        near_step(1 + k)
        if k < n_ccw:
            ccw.wait_recv()
            if k + 1 < n_ccw:
                ccw = zx_step(k + 1, -1)
            near_step(1 + n_cw + k)
        if k > 0:
            far_step(k - 1)
        for c in range(nx):
            zcw[c].wait_recv()
            if k + 1 < n_cw:
                zcw[c] = zs_step(k + 1, 1, c)
            if k < n_ccw:
                zccw[c].wait_recv()
                if k + 1 < n_ccw:
                    zccw[c] = zs_step(k + 1, -1, c)
    far_step(n_cw - 1)
    for copy in near[0] + near[1] + far:
        if copy is not None:
            copy.wait_recv()
    for copy in sent:
        copy.wait_send()
    loads.wait()

    at = lax.broadcasted_iota(jnp.int32, (LEN, 1), 0)
    halves = [(at0, min(cut, cols - at0)) for at0 in range(0, cols, cut)]

    def keep(value, mask):
        return jnp.where(mask, value.astype(F32), 0.0).astype(BF16)

    def tile(t, h):
        return x[pl.ds(t * LEN, LEN), pl.ds(*halves[h])]

    def inner(s, t, h):
        d = tab[s, t]
        if t == 0:
            z = jnp.where(at < d, tile(0, h), 0.0)
        elif t == SLOTS - 1:
            z = jnp.where(at >= d, tile(TILES - 1, h), 0.0)
        else:
            z = jnp.where(at >= d, tile(t - 1, h), tile(t, h))
        high, low = split(z)
        return dot(vt[s % 2, t], high) + dot(vt[s % 2, t], low)

    def scale(s, t, h, w):
        f = blocks[s, t, pl.ds(LEN, NB), :]
        y = dot(jnp.concatenate([f, f], axis=1), jnp.concatenate(split(w), axis=0))
        ys[s % 2, t, :, pl.ds(*halves[h])] = jnp.concatenate(split(y), axis=0)

    def apply(s, t, h):
        here = pl.ds(t * LEN, LEN), pl.ds(*halves[h])
        delta = dot(vpair[s % 2, t], ys[s % 2, pl.ds(t, 2), :, pl.ds(*halves[h])].reshape(4 * NB, halves[h][1]))
        x[here] = x[here] - delta

    def exchange(s, h):
        par = s % 2
        part = pl.ds(*halves[h])
        return [
            pltpu.make_async_remote_copy(
                src_ref=wbuf.at[par, side, :, part], dst_ref=wrec.at[par, 1 - side, :, part],
                send_sem=w_send.at[par, side, h], recv_sem=w_recv.at[par, 1 - side, h],
                device_id={"row": to}, device_id_type=MESH)
            for side, to in ((0, left_row), (1, right_row))
        ]

    def edges(s, h):
        wbuf[s % 2, 0, :, pl.ds(*halves[h])] = inner(s, 0, h)
        wbuf[s % 2, 1, :, pl.ds(*halves[h])] = inner(s, SLOTS - 1, h)
        for copy in exchange(s, h):
            copy.start()

    def finish(s, h):
        for copy in exchange(s, h):
            copy.wait()
        part = pl.ds(*halves[h])
        for side, t in ((0, 0), (1, SLOTS - 1)):
            scale(s, t, h, wbuf[s % 2, side, :, part] + wrec[s % 2, side, :, part])
        apply(s, 0, h)
        apply(s, TILES - 1, h)

    def begin(s):
        for t in range(SLOTS):
            vt[s % 2, t] = blocks[s, t, pl.ds(0, LEN), :].T
        for t in range(TILES):
            before = keep(blocks[s, t, pl.ds(0, LEN), :], at < tab[s, t])
            after = keep(blocks[s, t + 1, pl.ds(0, LEN), :], at >= tab[s, t + 1])
            vpair[s % 2, t] = jnp.concatenate([before, before, after, after], axis=1)

    def interior(s, h):
        for t in range(1, SLOTS - 1):
            scale(s, t, h, inner(s, t, h))
        for t in range(1, TILES - 1):
            apply(s, t, h)

    begin(0)
    for h in range(len(halves)):
        edges(0, h)
        interior(0, h)

    def sweep(s, carry):
        begin(s)
        for h in range(len(halves)):
            finish(s - 1, h)
            edges(s, h)
            interior(s, h)
        return carry

    lax.fori_loop(1, SWEEPS, sweep, 0)
    for h in range(len(halves)):
        finish(SWEEPS - 1, h)


def tables(offsets, owners):
    row, col = lax.axis_index("row"), lax.axis_index("col")
    begin_tile = offsets // LEN
    within = offsets % LEN
    slot = jnp.arange(8, dtype=jnp.int32) + (row * TILES - 1)
    slot = jnp.where(jnp.arange(8) < SLOTS, slot, -2)
    match = (begin_tile[:, None, :] == slot[None, :, None]).astype(jnp.int32)
    own = jnp.sum((owners == col) * within, axis=1, keepdims=True)
    return jnp.concatenate(
        [
            jnp.sum(match * within[:, None, :], axis=2),
            jnp.sum(match * owners[:, None, :], axis=2),
            jnp.sum(match, axis=2),
            jnp.broadcast_to(own, (SWEEPS, 8)),
        ],
        axis=1,
    ).astype(jnp.int32)


def on_device(nx, nz, nrow, slab, reflectors, factors, offsets, owners):
    cols = slab.shape[1]
    ncol = nx * nz
    dma = pltpu.SemaphoreType.DMA
    n_ring = nz - 1
    n_group = -(-cols // CUT)
    return pl.pallas_call(
        functools.partial(kernel, nx, nz, nrow, CUT),
        out_shape=pltpu.VMEM(slab.shape, F32),
        in_specs=[
            pl.BlockSpec(memory_space=pltpu.SMEM),
            pl.BlockSpec(memory_space=pl.ANY),
            pl.BlockSpec(memory_space=pltpu.VMEM),
            pl.BlockSpec(memory_space=pltpu.VMEM),
        ],
        out_specs=pl.BlockSpec(memory_space=pltpu.VMEM),
        scratch_shapes=[
            pltpu.VMEM((SWEEPS, BLK, NB), BF16),
            pltpu.VMEM((ncol, BLK // nz, NB), BF16),
            pltpu.VMEM((nx, SLOTS, BLK, NB), BF16),
            pltpu.VMEM((2, SLOTS, NB, LEN), BF16),
            pltpu.VMEM((2, TILES, LEN, 4 * NB), BF16),
            pltpu.VMEM((2, SLOTS, 2 * NB, cols), BF16),
            pltpu.VMEM((2, 2, NB, cols), F32),
            pltpu.VMEM((2, 2, NB, cols), F32),
            dma, dma((2,)),
            dma((n_ring,)), dma((n_ring,)),
            dma((2, nz)), dma((2, nz)),
            dma((nz,)), dma((nz,)),
            dma((nx - 1,)), dma((nx - 1,)),
            dma((n_ring, nx)), dma((n_ring, nx)),
            dma((2, 2, n_group)), dma((2, 2, n_group)),
        ],
        compiler_params=pltpu.CompilerParams(
            collective_id=0, has_side_effects=True, vmem_limit_bytes=56 * 2**20
        ),
        cost_estimate=pl.CostEstimate(flops=6_000_000_000, bytes_accessed=9_000_000, transcendentals=0),
    )(tables(offsets, owners), slab, reflectors, factors)


def solution(mesh):
    nx = SWEEPS
    nz = mesh.shape["col"] // nx
    placed = (P("row", "col"), P(None, "col", None, None), P(None, "col", None, None), P(), P())
    return jax.shard_map(
        functools.partial(on_device, nx, nz, mesh.shape["row"]),
        mesh=mesh, in_specs=placed, out_specs=P("row", "col"), check_vma=False,
    )
```

```python
import functools

import jax
import jax.numpy as jnp
from jax import lax
from jax.experimental import pallas as pl
from jax.experimental.pallas import tpu as pltpu
from jax.sharding import PartitionSpec as P

SWEEPS = 4
LEN = 256
NB = 128
SLOTS = 7
TILES = 6
ZX = 4
BLK = LEN + NB
CUT = 256
MESH = pl.DeviceIdType.MESH
F32 = jnp.float32
BF16 = jnp.bfloat16


def split(value):
    high = value.astype(BF16)
    low = (value - high.astype(F32)).astype(BF16)
    return high, low


def dot(left, right):
    return jnp.dot(left, right, preferred_element_type=F32)


def kernel(nx, nz, nrow, cut, offsets, owners, slab, refl, fact, x, tab, own, pieces, other, blocks, vt, vpair, ys, wbuf, wrec,
           load_sem, a2a_sem, pair_sem, zx_send, zx_recv, xs_send, xs_recv, far_send, far_recv, xz_send, xz_recv, zs_send, zs_recv,
           w_send, w_recv):
    ncol = nx * nz
    me = lax.axis_index("col")
    row = lax.axis_index("row")
    mx, mz = me // nz, me % nz
    piece = BLK // nz
    cols = x.shape[1]
    loads = pltpu.make_async_copy(slab, x, load_sem)
    loads.start()

    right_row, left_row = (row + 1) % nrow, (row + nrow - 1) % nrow
    barrier = pltpu.get_barrier_semaphore()

    def greet(k, carry):
        pl.semaphore_signal(barrier, inc=1, device_id={"col": (me + k) % ncol}, device_id_type=MESH)
        return carry

    lax.fori_loop(1, ncol, greet, 0)
    pl.semaphore_signal(barrier, inc=1, device_id={"row": right_row}, device_id_type=MESH)
    pl.semaphore_signal(barrier, inc=1, device_id={"row": left_row}, device_id_type=MESH)

    ri = lax.broadcasted_iota(jnp.int32, (LEN, LEN), 0)
    ci = lax.broadcasted_iota(jnp.int32, (LEN, LEN), 1)
    for s in range(SWEEPS):
        held = jnp.sum(jnp.where(owners[pl.ds(s, 1), :] == me, offsets[pl.ds(s, 1), :] & (LEN - 1), 0))
        place = (((ri - held) & (LEN - 1)) == ci).astype(BF16)
        own[s, pl.ds(0, LEN), :] = dot(place, refl[s, 0]).astype(BF16)
        own[s, pl.ds(LEN, NB), :] = fact[s, 0]

    def slot_of(s, t, of_row, value):
        begins_here = offsets[pl.ds(s, 1), :] // LEN == of_row * TILES + (t - 1)
        return jnp.sum(jnp.where(begins_here, value(pl.ds(s, 1)), 0))

    def within(s):
        return offsets[s, :] & (LEN - 1)

    def holder(s):
        return owners[s, :] + ncol

    for s in range(SWEEPS):
        for t in range(SLOTS):
            tab[s, t] = slot_of(s, t, row, within)
    core = row % 2
    sibling = row + 1 - 2 * core
    wanted = [[slot_of(mx, t, of_row, holder) for t in range(SLOTS)] for of_row in (row, sibling)]

    pl.semaphore_wait(barrier, ncol + 1)
    sender = mz % 2 == core

    def send_piece(k, carry):
        to = (me + k) % ncol
        pltpu.make_async_remote_copy(
            src_ref=own.at[to // nz, pl.ds(pl.multiple_of((to % nz) * piece, 16), piece), :],
            dst_ref=pieces.at[me // 2],
            send_sem=a2a_sem.at[2 * (k // pieces.shape[0])],
            recv_sem=a2a_sem.at[1],
            device_id={"col": to},
            device_id_type=MESH,
        ).start()
        return carry

    my_rows = pl.ds(pl.multiple_of(mz * piece, 16), piece)
    n_sent = pieces.shape[0]

    def await_pieces(count, sem):
        some = pieces.at[pl.ds(0, count)]
        pltpu.make_async_copy(some, some, sem).wait()

    @pl.when(sender)
    def _():
        lax.fori_loop(1, ncol, send_piece, 0)
        pieces[me // 2] = own[mx, my_rows, :]
        await_pieces(n_sent - 1, a2a_sem.at[1])

    @pl.when(jnp.logical_not(sender))
    def _():
        await_pieces(n_sent, a2a_sem.at[1])

    def found(at_holder):
        here = jnp.logical_and(at_holder >= ncol, at_holder % 2 == core)
        return pieces[(at_holder % ncol) // 2].astype(F32) * here.astype(F32)

    for t in range(SLOTS):
        other[0, t] = found(wanted[1][t]).astype(BF16)
    handed = pltpu.make_async_remote_copy(
        src_ref=other.at[0], dst_ref=other.at[1], send_sem=pair_sem.at[0], recv_sem=pair_sem.at[1],
        device_id={"row": sibling}, device_id_type=MESH)
    handed.start()
    mine_found = [found(wanted[0][t]) for t in range(SLOTS)]
    handed.wait_recv()
    for t in range(SLOTS):
        blocks[mx, t, my_rows, :] = (mine_found[t] + other[1, t].astype(F32)).astype(BF16)
    handed.wait_send()

    @pl.when(sender)
    def _():
        await_pieces(n_sent - 1, a2a_sem.at[0])
        await_pieces(n_sent, a2a_sem.at[2])

    def col_of(cx, cz):
        return ((cx + nx) % nx) * nz + (cz + nz) % nz

    def rows_of(cz):
        return pl.ds(pl.multiple_of(((cz + nz) % nz) * piece, 16), piece)

    def move(part, to, send, recv):
        copy = pltpu.make_async_remote_copy(
            src_ref=part, dst_ref=part, send_sem=send, recv_sem=recv, device_id={"col": to}, device_id_type=MESH)
        copy.start()
        return copy

    first = pl.ds(0, ZX)
    second = pl.ds(ZX, SLOTS - ZX)
    n_cw, n_ccw = nz // 2, (nz - 1) // 2
    reach = [0] + [-1 - k for k in range(n_cw)] + [1 + k for k in range(n_ccw)]
    sent = []

    def start(part, to, send, recv):
        copy = move(part, to, send, recv)
        sent.append(copy)
        return copy

    def zx_step(k, way):
        i = k if way > 0 else n_cw + k
        return start(blocks.at[mx, first, rows_of(mz - way * k), :], col_of(mx, mz + way), zx_send.at[i], zx_recv.at[i])

    def zs_step(k, way, c):
        i = k if way > 0 else n_cw + k
        part = blocks.at[c, second, rows_of(mz - way * k), :]
        return start(part, col_of(mx, mz + way), zs_send.at[i, c], zs_recv.at[i, c])

    near = [[None] * nz, [None] * nz]

    def near_step(i):
        part = blocks.at[mx, first, rows_of(mz + reach[i]), :]
        for side, way in ((0, 1), (1, -1)):
            near[side][i] = start(part, col_of(mx + way, mz), xs_send.at[side, i], xs_recv.at[side, i])

    order = [0] + [i for k in range(n_cw) for i in ((1 + k, 1 + n_cw + k) if k < n_ccw else (1 + k,))]
    far = []

    def far_step(j):
        for side, way in ((0, 1), (1, -1)):
            i = order[2 * j + side]
            near[side][i].wait_recv()
            near[side][i] = None
            part = blocks.at[(mx - way + nx) % nx, first, rows_of(mz + reach[i]), :]
            far.append(start(part, col_of(mx + way, mz), far_send.at[2 * j + side], far_recv.at[2 * j + side]))

    mine = blocks.at[mx, second, my_rows, :]
    xz = [start(mine, col_of(mx + k, mz), xz_send.at[k - 1], xz_recv.at[k - 1]) for k in range(1, nx)]
    cw = zx_step(0, 1)
    ccw = zx_step(0, -1) if n_ccw else None
    near_step(0)
    for copy in xz:
        copy.wait_recv()
    zcw, zccw = [None] * nx, [None] * nx
    for c in range(nx):
        zcw[c] = zs_step(0, 1, c)
        if n_ccw:
            zccw[c] = zs_step(0, -1, c)
    for k in range(n_cw):
        cw.wait_recv()
        if k + 1 < n_cw:
            cw = zx_step(k + 1, 1)
        near_step(1 + k)
        if k < n_ccw:
            ccw.wait_recv()
            if k + 1 < n_ccw:
                ccw = zx_step(k + 1, -1)
            near_step(1 + n_cw + k)
        if k > 0:
            far_step(k - 1)
        for c in range(nx):
            zcw[c].wait_recv()
            if k + 1 < n_cw:
                zcw[c] = zs_step(k + 1, 1, c)
            if k < n_ccw:
                zccw[c].wait_recv()
                if k + 1 < n_ccw:
                    zccw[c] = zs_step(k + 1, -1, c)
    far_step(n_cw - 1)
    for copy in near[0] + near[1] + far:
        if copy is not None:
            copy.wait_recv()
    for copy in sent:
        copy.wait_send()
    loads.wait()

    at = lax.broadcasted_iota(jnp.int32, (LEN, 1), 0)
    halves = [(at0, min(cut, cols - at0)) for at0 in range(0, cols, cut)]

    def keep(value, mask):
        return jnp.where(mask, value.astype(F32), 0.0).astype(BF16)

    def tile(t, h):
        return x[pl.ds(t * LEN, LEN), pl.ds(*halves[h])]

    def inner(s, t, h):
        d = tab[s, t]
        if t == 0:
            z = jnp.where(at < d, tile(0, h), 0.0)
        elif t == SLOTS - 1:
            z = jnp.where(at >= d, tile(TILES - 1, h), 0.0)
        else:
            z = jnp.where(at >= d, tile(t - 1, h), tile(t, h))
        return dot(vt[s % 2, t], jnp.concatenate(split(z), axis=0))

    def scale(s, slots, h, sums):
        y = []
        for t, w in zip(slots, sums):
            f = blocks[s, t, pl.ds(LEN, NB), :]
            y.append(dot(jnp.concatenate([f, f], axis=1), jnp.concatenate(split(w), axis=0)))
        for t, value in zip(slots, y):
            ys[s % 2, t, :, pl.ds(*halves[h])] = jnp.concatenate(split(value), axis=0)

    def apply(s, t, h):
        here = pl.ds(t * LEN, LEN), pl.ds(*halves[h])
        delta = dot(vpair[s % 2, t], ys[s % 2, pl.ds(t, 2), :, pl.ds(*halves[h])].reshape(4 * NB, halves[h][1]))
        x[here] = x[here] - delta

    def exchange(s, h):
        par = s % 2
        part = pl.ds(*halves[h])
        return [
            pltpu.make_async_remote_copy(
                src_ref=wbuf.at[par, side, :, part], dst_ref=wrec.at[par, 1 - side, :, part],
                send_sem=w_send.at[par, side, h], recv_sem=w_recv.at[par, 1 - side, h],
                device_id={"row": to}, device_id_type=MESH)
            for side, to in ((0, left_row), (1, right_row))
        ]

    def edges(s, h):
        first_sum, last_sum = inner(s, 0, h), inner(s, SLOTS - 1, h)
        wbuf[s % 2, 0, :, pl.ds(*halves[h])] = first_sum
        wbuf[s % 2, 1, :, pl.ds(*halves[h])] = last_sum
        for copy in exchange(s, h):
            copy.start()

    def finish(s, h):
        for copy in exchange(s, h):
            copy.wait()
        part = pl.ds(*halves[h])
        scale(s, (0, SLOTS - 1), h, [wbuf[s % 2, side, :, part] + wrec[s % 2, side, :, part] for side in (0, 1)])
        apply(s, 0, h)
        apply(s, TILES - 1, h)

    def begin(s):
        for t in range(SLOTS):
            turned = blocks[s, t, pl.ds(0, LEN), :].T
            vt[s % 2, t] = jnp.concatenate([turned, turned], axis=1)
        for t in range(TILES):
            before = keep(blocks[s, t, pl.ds(0, LEN), :], at < tab[s, t])
            after = keep(blocks[s, t + 1, pl.ds(0, LEN), :], at >= tab[s, t + 1])
            vpair[s % 2, t] = jnp.concatenate([before, before, after, after], axis=1)

    def interior(s, h):
        scale(s, range(1, SLOTS - 1), h, [inner(s, t, h) for t in range(1, SLOTS - 1)])
        for t in range(1, TILES - 1):
            apply(s, t, h)

    begin(0)
    for h in range(len(halves)):
        edges(0, h)
        interior(0, h)

    def sweep(s, carry):
        begin(s)
        for h in range(len(halves)):
            finish(s - 1, h)
            edges(s, h)
            interior(s, h)
        return carry

    lax.fori_loop(1, SWEEPS, sweep, 0)
    for h in range(len(halves)):
        finish(SWEEPS - 1, h)


def on_device(nx, nz, nrow, slab, reflectors, factors, offsets, owners):
    cols = slab.shape[1]
    ncol = nx * nz
    dma = pltpu.SemaphoreType.DMA
    n_ring = nz - 1
    n_group = -(-cols // CUT)
    return pl.pallas_call(
        functools.partial(kernel, nx, nz, nrow, CUT),
        out_shape=pltpu.VMEM(slab.shape, F32),
        in_specs=[
            pl.BlockSpec(memory_space=pltpu.VMEM),
            pl.BlockSpec(memory_space=pltpu.VMEM),
            pl.BlockSpec(memory_space=pl.ANY),
            pl.BlockSpec(memory_space=pltpu.VMEM),
            pl.BlockSpec(memory_space=pltpu.VMEM),
        ],
        out_specs=pl.BlockSpec(memory_space=pltpu.VMEM),
        scratch_shapes=[
            pltpu.SMEM((SWEEPS, 8), jnp.int32),
            pltpu.VMEM((SWEEPS, BLK, NB), BF16),
            pltpu.VMEM((ncol // 2, BLK // nz, NB), BF16),
            pltpu.VMEM((2, SLOTS, BLK // nz, NB), BF16),
            pltpu.VMEM((nx, SLOTS, BLK, NB), BF16),
            pltpu.VMEM((2, SLOTS, NB, 2 * LEN), BF16),
            pltpu.VMEM((2, TILES, LEN, 4 * NB), BF16),
            pltpu.VMEM((2, SLOTS, 2 * NB, cols), BF16),
            pltpu.VMEM((2, 2, NB, cols), F32),
            pltpu.VMEM((2, 2, NB, cols), F32),
            dma, dma((3,)), dma((2,)),
            dma((n_ring,)), dma((n_ring,)),
            dma((2, nz)), dma((2, nz)),
            dma((nz,)), dma((nz,)),
            dma((nx - 1,)), dma((nx - 1,)),
            dma((n_ring, nx)), dma((n_ring, nx)),
            dma((2, 2, n_group)), dma((2, 2, n_group)),
        ],
        compiler_params=pltpu.CompilerParams(
            collective_id=0, has_side_effects=True, vmem_limit_bytes=56 * 2**20
        ),
        cost_estimate=pl.CostEstimate(flops=6_000_000_000, bytes_accessed=9_000_000, transcendentals=0),
    )(offsets, owners, slab, reflectors, factors)


def solution(mesh):
    nx = SWEEPS
    nz = mesh.shape["col"] // nx
    placed = (P("row", "col"), P(None, "col", None, None), P(None, "col", None, None), P(), P())
    return jax.shard_map(
        functools.partial(on_device, nx, nz, mesh.shape["row"]),
        mesh=mesh, in_specs=placed, out_specs=P("row", "col"), check_vma=False,
    )
```

```python
import functools

import jax
import jax.numpy as jnp
from jax import lax
from jax.experimental import pallas as pl
from jax.experimental.pallas import tpu as pltpu
from jax.sharding import PartitionSpec as P

SWEEPS = 4
LEN = 256
NB = 128
SLOTS = 7
TILES = 6
ZX = 5
BLK = LEN + NB
CUT = 256
MESH = pl.DeviceIdType.MESH
F32 = jnp.float32
BF16 = jnp.bfloat16


def split(value):
    high = value.astype(BF16)
    low = (value - high.astype(F32)).astype(BF16)
    return high, low


def dot(left, right):
    return jnp.dot(left, right, preferred_element_type=F32)


def kernel(nx, nz, nrow, cut, offsets, owners, slab, refl, fact, x, tab, own, pieces, other, blocks, vt, vpair, ys, wbuf, wrec,
           load_sem, a2a_sem, pair_sem, zx_send, zx_recv, xs_send, xs_recv, far_send, far_recv, xz_send, xz_recv, zs_send, zs_recv,
           w_send, w_recv):
    ncol = nx * nz
    me = lax.axis_index("col")
    row = lax.axis_index("row")
    mx, mz = me // nz, me % nz
    piece = BLK // nz
    cols = x.shape[1]
    loads = pltpu.make_async_copy(slab, x, load_sem)
    loads.start()

    right_row, left_row = (row + 1) % nrow, (row + nrow - 1) % nrow
    barrier = pltpu.get_barrier_semaphore()

    def greet(k, carry):
        pl.semaphore_signal(barrier, inc=1, device_id={"col": (me + k) % ncol}, device_id_type=MESH)
        return carry

    lax.fori_loop(1, ncol, greet, 0)
    pl.semaphore_signal(barrier, inc=1, device_id={"row": right_row}, device_id_type=MESH)
    pl.semaphore_signal(barrier, inc=1, device_id={"row": left_row}, device_id_type=MESH)

    ri = lax.broadcasted_iota(jnp.int32, (LEN, LEN), 0)
    ci = lax.broadcasted_iota(jnp.int32, (LEN, LEN), 1)
    for s in range(SWEEPS):
        held = jnp.sum(jnp.where(owners[pl.ds(s, 1), :] == me, offsets[pl.ds(s, 1), :] & (LEN - 1), 0))
        place = (((ri - held) & (LEN - 1)) == ci).astype(BF16)
        own[s, pl.ds(0, LEN), :] = dot(place, refl[s, 0]).astype(BF16)
        own[s, pl.ds(LEN, NB), :] = fact[s, 0]

    def slot_of(s, t, of_row, value):
        begins_here = offsets[pl.ds(s, 1), :] // LEN == of_row * TILES + (t - 1)
        return jnp.sum(jnp.where(begins_here, value(pl.ds(s, 1)), 0))

    def within(s):
        return offsets[s, :] & (LEN - 1)

    def holder(s):
        return owners[s, :] + ncol

    for s in range(SWEEPS):
        for t in range(SLOTS):
            tab[s, t] = slot_of(s, t, row, within)
    core = row % 2
    sibling = row + 1 - 2 * core
    wanted = [[slot_of(mx, t, of_row, holder) for t in range(SLOTS)] for of_row in (row, sibling)]

    pl.semaphore_wait(barrier, ncol + 1)
    sender = mz % 2 == core

    def send_piece(k, carry):
        to = (me + k) % ncol
        pltpu.make_async_remote_copy(
            src_ref=own.at[to // nz, pl.ds(pl.multiple_of((to % nz) * piece, 16), piece), :],
            dst_ref=pieces.at[me // 2],
            send_sem=a2a_sem.at[2 * (k // pieces.shape[0])],
            recv_sem=a2a_sem.at[1],
            device_id={"col": to},
            device_id_type=MESH,
        ).start()
        return carry

    my_rows = pl.ds(pl.multiple_of(mz * piece, 16), piece)
    n_sent = pieces.shape[0]

    def await_pieces(count, sem):
        some = pieces.at[pl.ds(0, count)]
        pltpu.make_async_copy(some, some, sem).wait()

    @pl.when(sender)
    def _():
        lax.fori_loop(1, ncol, send_piece, 0)
        pieces[me // 2] = own[mx, my_rows, :]
        await_pieces(n_sent - 1, a2a_sem.at[1])

    @pl.when(jnp.logical_not(sender))
    def _():
        await_pieces(n_sent, a2a_sem.at[1])

    def found(at_holder):
        here = jnp.logical_and(at_holder >= ncol, at_holder % 2 == core)
        return pieces[(at_holder % ncol) // 2].astype(F32) * here.astype(F32)

    for t in range(SLOTS):
        other[0, t] = found(wanted[1][t]).astype(BF16)
    handed = pltpu.make_async_remote_copy(
        src_ref=other.at[0], dst_ref=other.at[1], send_sem=pair_sem.at[0], recv_sem=pair_sem.at[1],
        device_id={"row": sibling}, device_id_type=MESH)
    handed.start()
    mine_found = [found(wanted[0][t]) for t in range(SLOTS)]
    handed.wait_recv()
    for t in range(SLOTS):
        blocks[mx, t, my_rows, :] = (mine_found[t] + other[1, t].astype(F32)).astype(BF16)
    handed.wait_send()

    @pl.when(sender)
    def _():
        await_pieces(n_sent - 1, a2a_sem.at[0])
        await_pieces(n_sent, a2a_sem.at[2])

    def col_of(cx, cz):
        return ((cx + nx) % nx) * nz + (cz + nz) % nz

    def rows_of(cz):
        return pl.ds(pl.multiple_of(((cz + nz) % nz) * piece, 16), piece)

    def move(part, to, send, recv):
        copy = pltpu.make_async_remote_copy(
            src_ref=part, dst_ref=part, send_sem=send, recv_sem=recv, device_id={"col": to}, device_id_type=MESH)
        copy.start()
        return copy

    first = pl.ds(0, ZX)
    second = pl.ds(ZX, SLOTS - ZX)
    n_cw, n_ccw = nz // 2, (nz - 1) // 2
    reach = [0] + [-1 - k for k in range(n_cw)] + [1 + k for k in range(n_ccw)]
    sent = []

    def start(part, to, send, recv):
        copy = move(part, to, send, recv)
        sent.append(copy)
        return copy

    def zx_step(k, way):
        i = k if way > 0 else n_cw + k
        return start(blocks.at[mx, first, rows_of(mz - way * k), :], col_of(mx, mz + way), zx_send.at[i], zx_recv.at[i])

    def zs_step(k, way, c):
        i = k if way > 0 else n_cw + k
        part = blocks.at[c, second, rows_of(mz - way * k), :]
        return start(part, col_of(mx, mz + way), zs_send.at[i, c], zs_recv.at[i, c])

    near = [[None] * nz, [None] * nz]

    def near_step(i):
        part = blocks.at[mx, first, rows_of(mz + reach[i]), :]
        for side, way in ((0, 1), (1, -1)):
            near[side][i] = start(part, col_of(mx + way, mz), xs_send.at[side, i], xs_recv.at[side, i])

    order = [0] + [i for k in range(n_cw) for i in ((1 + k, 1 + n_cw + k) if k < n_ccw else (1 + k,))]
    far = []

    def far_step(j):
        for side, way in ((0, 1), (1, -1)):
            i = order[2 * j + side]
            near[side][i].wait_recv()
            near[side][i] = None
            part = blocks.at[(mx - way + nx) % nx, first, rows_of(mz + reach[i]), :]
            far.append(start(part, col_of(mx + way, mz), far_send.at[2 * j + side], far_recv.at[2 * j + side]))

    mine = blocks.at[mx, second, my_rows, :]
    xz = [start(mine, col_of(mx + k, mz), xz_send.at[k - 1], xz_recv.at[k - 1]) for k in range(1, nx)]
    cw = zx_step(0, 1)
    ccw = zx_step(0, -1) if n_ccw else None
    near_step(0)
    for copy in xz:
        copy.wait_recv()
    zcw, zccw = [None] * nx, [None] * nx
    for c in range(nx):
        zcw[c] = zs_step(0, 1, c)
        if n_ccw:
            zccw[c] = zs_step(0, -1, c)
    for k in range(n_cw):
        cw.wait_recv()
        if k + 1 < n_cw:
            cw = zx_step(k + 1, 1)
        near_step(1 + k)
        if k < n_ccw:
            ccw.wait_recv()
            if k + 1 < n_ccw:
                ccw = zx_step(k + 1, -1)
            near_step(1 + n_cw + k)
        if k > 0:
            far_step(k - 1)
        for c in range(nx):
            zcw[c].wait_recv()
            if k + 1 < n_cw:
                zcw[c] = zs_step(k + 1, 1, c)
            if k < n_ccw:
                zccw[c].wait_recv()
                if k + 1 < n_ccw:
                    zccw[c] = zs_step(k + 1, -1, c)
    far_step(n_cw - 1)
    for copy in near[0] + near[1] + far:
        if copy is not None:
            copy.wait_recv()
    loads.wait()

    at = lax.broadcasted_iota(jnp.int32, (LEN, 1), 0)
    halves = [(at0, min(cut, cols - at0)) for at0 in range(0, cols, cut)]

    def keep(value, mask):
        return jnp.where(mask, value.astype(F32), 0.0).astype(BF16)

    def tile(t, h):
        return x[pl.ds(t * LEN, LEN), pl.ds(*halves[h])]

    def inner(s, t, h):
        d = tab[s, t]
        if t == 0:
            z = jnp.where(at < d, tile(0, h), 0.0)
        elif t == SLOTS - 1:
            z = jnp.where(at >= d, tile(TILES - 1, h), 0.0)
        else:
            z = jnp.where(at >= d, tile(t - 1, h), tile(t, h))
        return dot(vt[s % 2, t], jnp.concatenate(split(z), axis=0))

    def scale(s, slots, h, sums):
        y = []
        for t, w in zip(slots, sums):
            f = blocks[s, t, pl.ds(LEN, NB), :]
            y.append(dot(jnp.concatenate([f, f], axis=1), jnp.concatenate(split(w), axis=0)))
        for t, value in zip(slots, y):
            ys[s % 2, t, :, pl.ds(*halves[h])] = jnp.concatenate(split(value), axis=0)

    def apply(s, t, h):
        here = pl.ds(t * LEN, LEN), pl.ds(*halves[h])
        delta = dot(vpair[s % 2, t], ys[s % 2, pl.ds(t, 2), :, pl.ds(*halves[h])].reshape(4 * NB, halves[h][1]))
        x[here] = x[here] - delta

    def exchange(s, h):
        par = s % 2
        part = pl.ds(*halves[h])
        return [
            pltpu.make_async_remote_copy(
                src_ref=wbuf.at[par, side, :, part], dst_ref=wrec.at[par, 1 - side, :, part],
                send_sem=w_send.at[par, side, h], recv_sem=w_recv.at[par, 1 - side, h],
                device_id={"row": to}, device_id_type=MESH)
            for side, to in ((0, left_row), (1, right_row))
        ]

    def edges(s, h):
        first_sum, last_sum = inner(s, 0, h), inner(s, SLOTS - 1, h)
        wbuf[s % 2, 0, :, pl.ds(*halves[h])] = first_sum
        wbuf[s % 2, 1, :, pl.ds(*halves[h])] = last_sum
        for copy in exchange(s, h):
            copy.start()

    def finish(s, h):
        for copy in exchange(s, h):
            copy.wait()
        part = pl.ds(*halves[h])
        scale(s, (0, SLOTS - 1), h, [wbuf[s % 2, side, :, part] + wrec[s % 2, side, :, part] for side in (0, 1)])
        apply(s, 0, h)
        apply(s, TILES - 1, h)

    def begin(s):
        for t in range(SLOTS):
            turned = blocks[s, t, pl.ds(0, LEN), :].T
            vt[s % 2, t] = jnp.concatenate([turned, turned], axis=1)
        for t in range(TILES):
            before = keep(blocks[s, t, pl.ds(0, LEN), :], at < tab[s, t])
            after = keep(blocks[s, t + 1, pl.ds(0, LEN), :], at >= tab[s, t + 1])
            vpair[s % 2, t] = jnp.concatenate([before, before, after, after], axis=1)

    def interior(s, h):
        scale(s, range(1, SLOTS - 1), h, [inner(s, t, h) for t in range(1, SLOTS - 1)])
        for t in range(1, TILES - 1):
            apply(s, t, h)

    begin(0)
    for h in range(len(halves)):
        edges(0, h)
        interior(0, h)

    def sweep(s, carry):
        begin(s)
        for h in range(len(halves)):
            finish(s - 1, h)
            edges(s, h)
            interior(s, h)
        return carry

    lax.fori_loop(1, SWEEPS, sweep, 0)
    for h in range(len(halves)):
        finish(SWEEPS - 1, h)
    for copy in sent:
        copy.wait_send()


def on_device(nx, nz, nrow, slab, reflectors, factors, offsets, owners):
    cols = slab.shape[1]
    ncol = nx * nz
    dma = pltpu.SemaphoreType.DMA
    n_ring = nz - 1
    n_group = -(-cols // CUT)
    return pl.pallas_call(
        functools.partial(kernel, nx, nz, nrow, CUT),
        out_shape=pltpu.VMEM(slab.shape, F32),
        in_specs=[
            pl.BlockSpec(memory_space=pltpu.VMEM),
            pl.BlockSpec(memory_space=pltpu.VMEM),
            pl.BlockSpec(memory_space=pl.ANY),
            pl.BlockSpec(memory_space=pltpu.VMEM),
            pl.BlockSpec(memory_space=pltpu.VMEM),
        ],
        out_specs=pl.BlockSpec(memory_space=pltpu.VMEM),
        scratch_shapes=[
            pltpu.SMEM((SWEEPS, 8), jnp.int32),
            pltpu.VMEM((SWEEPS, BLK, NB), BF16),
            pltpu.VMEM((ncol // 2, BLK // nz, NB), BF16),
            pltpu.VMEM((2, SLOTS, BLK // nz, NB), BF16),
            pltpu.VMEM((nx, SLOTS, BLK, NB), BF16),
            pltpu.VMEM((2, SLOTS, NB, 2 * LEN), BF16),
            pltpu.VMEM((2, TILES, LEN, 4 * NB), BF16),
            pltpu.VMEM((2, SLOTS, 2 * NB, cols), BF16),
            pltpu.VMEM((2, 2, NB, cols), F32),
            pltpu.VMEM((2, 2, NB, cols), F32),
            dma, dma((3,)), dma((2,)),
            dma((n_ring,)), dma((n_ring,)),
            dma((2, nz)), dma((2, nz)),
            dma((nz,)), dma((nz,)),
            dma((nx - 1,)), dma((nx - 1,)),
            dma((n_ring, nx)), dma((n_ring, nx)),
            dma((2, 2, n_group)), dma((2, 2, n_group)),
        ],
        compiler_params=pltpu.CompilerParams(
            collective_id=0, has_side_effects=True, vmem_limit_bytes=56 * 2**20
        ),
        cost_estimate=pl.CostEstimate(flops=6_000_000_000, bytes_accessed=9_000_000, transcendentals=0),
    )(offsets, owners, slab, reflectors, factors)


def solution(mesh):
    nx = SWEEPS
    nz = mesh.shape["col"] // nx
    placed = (P("row", "col"), P(None, "col", None, None), P(None, "col", None, None), P(), P())
    return jax.shard_map(
        functools.partial(on_device, nx, nz, mesh.shape["row"]),
        mesh=mesh, in_specs=placed, out_specs=P("row", "col"), check_vma=False,
    )
```
